256 devices in a mesh: fsdp: 8 (over z), rep: 32 (over x, y, core).
Axes of the slice: x: 4, y: 4, z: 8, core: 2. Of those that a mesh axis runs over, the one named last changes fastest.
Arguments:
- grads: bfloat16 [32, 8192, 512], P('rep', 'fsdp'), may hold values from -120 to 120
- errors: bfloat16 [32, 8192, 512], P('rep', 'fsdp'), may hold values from -4 to 4
- q_prev: float32 [512, 64], replicated, may hold values from -6 to 6
- weight: float32 [8192, 512], P('fsdp'), may hold values from -4 to 4
- first_moment: bfloat16 [8192, 512], P('fsdp'), may hold values from -0.59765625 to 0.59765625
- second_moment: bfloat16 [8192, 512], P('fsdp'), may hold values from 0.0029907227 to 0.029907227
Outputs:
- new_errors: bfloat16 [32, 8192, 512], P('rep', 'fsdp')
- q_next: float32 [512, 64], replicated
- new_weight: float32 [8192, 512], P('fsdp')
- new_first: bfloat16 [8192, 512], P('fsdp')
- new_second: bfloat16 [8192, 512], P('fsdp')
The draws below stay inside these ranges and needn't reach their ends.
All inputs are finite; a program needn't handle non-finite values.
Results may differ from the reference program's by a relative error of at most 0.0018.
Values sent between devices are 32-bit elements; how exact they have to be, the bound alone decides.
No kernel may reach another device: no remote copies, remote signals or barrier semaphores. Data moves between devices by JAX's collectives and lax.ppermute only.
A program may use at most 64 MiB of HBM per device.

```python
import math
import jax
import jax.numpy as jnp
from jax import lax

D = 8192
COLS = 512
R = 64
REPLICAS = 32
N_REP = 32


def draw_grads(key, part):
    key = jax.random.fold_in(key, 11)
    row_key, col_key, noise_key = jax.random.split(key, 3)
    ramp = 3.0 ** (jnp.arange(D, dtype=jnp.float32) / D)
    row_scale = ramp * jnp.exp(jax.random.uniform(row_key, (D,), jnp.float32, -1.15, 1.15))
    col_scale = jnp.exp(jax.random.uniform(col_key, (COLS,), jnp.float32, -1.15, 1.15))
    values = jax.random.truncated_normal(noise_key, -4.0, 4.0, (REPLICAS, D, COLS), jnp.float32)
    return (values * row_scale[None, :, None] * col_scale[None, None, :]).astype(jnp.bfloat16)


def block_levels(rng, dims, pieces, low, top_value):
    loudness, own = 1.0, jax.random.fold_in(rng, 6)
    for axis_at, shards_of in pieces:
        steps = jnp.exp(jax.random.uniform(jax.random.fold_in(own, axis_at), (shards_of,), jnp.float32, low / len(pieces), top_value / len(pieces)))
        loudness = loudness * jnp.repeat(steps, dims[axis_at] // shards_of).reshape([-1 if axis == axis_at else 1 for axis in range(len(dims))])
    return loudness


def scatter_about(key, extent, width, reach, cuts=(), held_as=jnp.bfloat16):
    level = block_levels(key, extent, cuts, -0.22, 0.18) if cuts else 1.0
    result = jax.random.normal(key, extent, jnp.float32) * width * level
    return jnp.minimum(jnp.maximum(result, -reach), reach).astype(held_as)


def setup_inputs(seed: int = 0) -> dict:
    key_list = jax.random.split(jax.random.key(seed), 7)
    grads = draw_grads(jax.random.fold_in(key_list[6], 71), 0)
    errors = scatter_about(key_list[1], (REPLICAS, D, COLS), 0.5, 4.0, ((0, 32), (1, 8)))
    q_prev = scatter_about(key_list[2], (COLS, R), 1.0, 6.0, (), jnp.float32)
    weight = scatter_about(key_list[3], (D, COLS), 0.5, 4.0, ((0, 8),), jnp.float32)
    first_moment = scatter_about(key_list[4], (D, COLS), 0.1, 0.59765625, ((0, 8),))
    second_moment = jnp.clip(jnp.exp(math.log(0.029907227) - 2.3025851 * jax.random.uniform(key_list[5], (D, COLS), jnp.float32) ** block_levels(key_list[5], (D, COLS), ((0, 8),), -0.2, 0.2)), 0.0029907227, 0.029907227).astype(jnp.bfloat16)
    return {"grads": grads, "errors": errors, "q_prev": q_prev, "weight": weight, "first_moment": first_moment, "second_moment": second_moment}


beta_first = 0.9
beta_second = 0.95
learn_rate = 0.05
weight_decay = 0.1
epsilon = 1e-08
correct_first = 1.0 - 0.9 ** 10
correct_second = 1.0 - 0.95 ** 10

def merge_pair(inputs_pair):
    return inputs_pair[0].astype(jnp.float32) + inputs_pair[1].astype(jnp.float32)

def reference(grads, errors, q_prev, weight, first_moment, second_moment):

    def left_term(inputs_pair):
        return jnp.dot(merge_pair(inputs_pair).astype(jnp.float32), q_prev.astype(jnp.float32), precision=lax.Precision.HIGHEST, preferred_element_type=jnp.float32)
    factor = lax.optimization_barrier(jnp.sum(lax.map(left_term, (grads, errors)), axis=0))
    gram_matrix = jnp.dot(factor.T.astype(jnp.float32), factor.astype(jnp.float32), precision=lax.Precision.HIGHEST, preferred_element_type=jnp.float32)
    triangle = jnp.linalg.cholesky(gram_matrix)
    ortho_basis = lax.linalg.triangular_solve(triangle, factor, left_side=False, lower=True, transpose_a=True)

    def right_term(inputs_pair):
        return lax.dot_general(merge_pair(inputs_pair).astype(jnp.float32), ortho_basis.astype(jnp.float32), (((0,), (0,)), ((), ())), precision=lax.Precision.HIGHEST, preferred_element_type=jnp.float32)
    q_next = lax.optimization_barrier(jnp.sum(lax.map(right_term, (grads, errors)), axis=0)) / N_REP
    approx = jnp.dot(ortho_basis.astype(jnp.float32), q_next.T.astype(jnp.float32), precision=lax.Precision.HIGHEST, preferred_element_type=jnp.float32)

    def error_term(inputs_pair):
        return (merge_pair(inputs_pair) - approx).astype(jnp.bfloat16)
    new_errors = lax.map(error_term, (grads, errors))
    first_f = beta_first * first_moment.astype(jnp.float32) + (1.0 - beta_first) * approx
    second_f = beta_second * second_moment.astype(jnp.float32) + (1.0 - beta_second) * approx * approx
    adam_ratio = first_f / correct_first / (jnp.sqrt(second_f / correct_second) + epsilon)
    new_weight = weight - learn_rate * (adam_ratio + weight_decay * weight)
    return (new_errors, q_next, new_weight, first_f.astype(jnp.bfloat16), second_f.astype(jnp.bfloat16))
```

```python
import functools

import jax
import jax.numpy as jnp
from jax import lax
from jax.experimental import pallas as pl
from jax.experimental.pallas import tpu as pltpu
from jax.sharding import PartitionSpec as P

beta_first = 0.9
beta_second = 0.95
learn_rate = 0.05
weight_decay = 0.1
epsilon = 1e-08
correct_first = 1.0 - 0.9**10
correct_second = 1.0 - 0.95**10

ROWS, COLS, RANK, N_REP, N_FSDP = 1024, 512, 64, 32, 8
LANES = 128
f32, bf16 = jnp.float32, jnp.bfloat16
NT = (((1,), (1,)), ((), ()))
NN = (((1,), (0,)), ((), ()))
TN = (((0,), (0,)), ((), ()))


def mm(a, b, dims):
    return lax.dot_general(a, b, dims, preferred_element_type=f32)


def split3(x):
    hi = x.astype(bf16)
    rest = x - hi.astype(f32)
    mid = rest.astype(bf16)
    lo = (rest - mid.astype(f32)).astype(bf16)
    return hi, mid, lo


def stack3(x):
    return jnp.concatenate(split3(x), axis=0)


def fold3(x):
    n = x.shape[0] // 3
    return x[:n] + x[n : 2 * n] + x[2 * n :]


def exact(a, b, dims):
    a1, a2, a3 = split3(a)
    b1, b2, b3 = split3(b)
    small = mm(a1, b3, dims) + mm(a3, b1, dims) + mm(a2, b2, dims)
    return small + (mm(a1, b2, dims) + mm(a2, b1, dims)) + mm(a1, b1, dims)


LEFT_STEP = 256


def left_body(grads, errors, q_prev, out, q_parts):
    @pl.when(pl.program_id(0) == 0)
    def _():
        q_parts[...] = stack3(q_prev[...])

    q = q_parts[...]
    block = fold3(mm(q, grads[0], NT) + mm(q, errors[0], NT))
    for k in range(LEFT_STEP // LANES):
        out[k] = block[:, k * LANES : (k + 1) * LANES]


def left_factor(grads, errors, q_prev):
    steps = ROWS // LEFT_STEP
    rows = pl.BlockSpec((1, LEFT_STEP, COLS), lambda i: (0, i, 0))
    return pl.pallas_call(
        left_body,
        grid=(steps,),
        in_specs=[rows, rows, pl.BlockSpec((RANK, COLS), lambda i: (0, 0))],
        out_specs=pl.BlockSpec((LEFT_STEP // LANES, RANK, LANES), lambda i: (i, 0, 0)),
        out_shape=jax.ShapeDtypeStruct((ROWS // LANES, RANK, LANES), f32),
        scratch_shapes=[pltpu.VMEM((3 * RANK, COLS), bf16)],
        name="left_factor",
    )(grads, errors, q_prev.T)


def sum_copies_body(copies, pieces, out):
    total = pieces[0]
    for k in range(1, pieces.shape[0]):
        total = total + pieces[k]
    for k in range(copies):
        out[k] = total


def sum_copies(pieces, copies):
    return pl.pallas_call(
        functools.partial(sum_copies_body, copies),
        out_shape=jax.ShapeDtypeStruct((copies, *pieces.shape[1:]), f32),
        name="sum_copies",
    )(pieces)


def right_body(grads, errors, factor, out, acc, gram):
    step = pl.program_id(0)
    parts = stack3(jnp.concatenate([factor[k] for k in range(factor.shape[0])], axis=1))
    right = fold3(mm(parts, grads[0], NN) + mm(parts, errors[0], NN))
    square = fold3(mm(parts, parts, NT))
    square = square[:, :RANK] + square[:, RANK : 2 * RANK] + square[:, 2 * RANK :]

    @pl.when(step == 0)
    def _():
        acc[...] = right
        gram[...] = square

    @pl.when(step > 0)
    def _():
        acc[...] += right
        gram[...] += square

    @pl.when(step == pl.num_programs(0) - 1)
    def _():
        for c in range(N_REP):
            i, j = divmod(c, COLS // LANES)
            out[c, :8] = acc[8 * i : 8 * i + 8, LANES * j : LANES * (j + 1)]
            out[c, 8:] = jnp.zeros((8, LANES), f32)
        for c in range(RANK // 8):
            out[c, 8:, :RANK] = gram[8 * c : 8 * c + 8, :] * (1.0 / N_REP)


def right_term(grads, errors, factor):
    steps = 4
    n = ROWS // steps
    rows = pl.BlockSpec((1, n, COLS), lambda i: (0, i, 0))
    return pl.pallas_call(
        right_body,
        grid=(steps,),
        in_specs=[rows, rows, pl.BlockSpec((n // LANES, RANK, LANES), lambda i: (i, 0, 0))],
        out_specs=pl.BlockSpec((N_REP, 16, LANES), lambda i: (0, 0, 0)),
        out_shape=jax.ShapeDtypeStruct((N_REP, 16, LANES), f32),
        scratch_shapes=[pltpu.VMEM((RANK, COLS), f32), pltpu.VMEM((RANK, RANK), f32)],
        name="right_term",
    )(grads, errors, factor)


def inverse_triangle(gram):
    eye = (
        lax.broadcasted_iota(jnp.int32, (RANK, RANK), 0)
        == lax.broadcasted_iota(jnp.int32, (RANK, RANK), 1)
    ).astype(f32)
    both = jnp.concatenate([gram, eye], axis=1)
    below = lax.broadcasted_iota(jnp.int32, (RANK, 1), 0)
    roots = jnp.zeros((RANK, 1), f32)
    for k in range(RANK):
        pivot_row = both[k : k + 1, :]
        column = both[:, k : k + 1]
        pivot = pivot_row[:, k : k + 1]
        roots = jnp.where(below == k, lax.rsqrt(pivot), roots)
        scale = jnp.where(below > k, column / pivot, 0.0)
        both = both - scale * pivot_row
    return both[:, RANK:] * roots


def final_body(
    grads, errors, factor, sums, weight, first, second,
    new_errors, q_next, new_weight, new_first, new_second, mix,
):
    @pl.when(pl.program_id(0) == 0)
    def _():
        gram = jnp.concatenate([sums[c, 8:, :RANK] for c in range(RANK // 8)], axis=0)
        wide = COLS // LANES
        right = jnp.concatenate(
            [
                jnp.concatenate([sums[i * wide + j, :8] for j in range(wide)], axis=1)
                for i in range(RANK // 8)
            ],
            axis=0,
        )
        inverse = inverse_triangle(gram)
        q_t = exact(inverse, right, NN) * (1.0 / N_REP)
        q_next[...] = q_t
        w1, w2, w3 = split3(exact(inverse, q_t, TN))
        mix[...] = jnp.concatenate([w1, w2, w1, w3, w2, w1], axis=0)

    f1, f2, f3 = split3(factor[0])
    approx = mm(jnp.concatenate([f1, f1, f2, f1, f2, f3], axis=0), mix[...], TN)
    merged = grads[0].astype(f32) + errors[0].astype(f32)
    new_errors[0] = (merged - approx).astype(bf16)
    first_f = beta_first * first[...].astype(f32) + (1.0 - beta_first) * approx
    second_f = beta_second * second[...].astype(f32) + (1.0 - beta_second) * approx * approx
    ratio = first_f / correct_first / (jnp.sqrt(second_f / correct_second) + epsilon)
    w = weight[...]
    new_weight[...] = w - learn_rate * (ratio + weight_decay * w)
    new_first[...] = first_f.astype(bf16)
    new_second[...] = second_f.astype(bf16)


def final(grads, errors, factor, sums, weight, first, second):
    n = LANES
    rows3 = pl.BlockSpec((1, n, COLS), lambda i: (0, i, 0))
    rows2 = pl.BlockSpec((n, COLS), lambda i: (i, 0))
    return pl.pallas_call(
        final_body,
        grid=(ROWS // n,),
        in_specs=[
            rows3, rows3,
            pl.BlockSpec((1, RANK, LANES), lambda i: (i, 0, 0)),
            pl.BlockSpec((N_REP, 16, LANES), lambda i: (0, 0, 0)),
            rows2, rows2, rows2,
        ],
        out_specs=[rows3, pl.BlockSpec((RANK, COLS), lambda i: (0, 0)), rows2, rows2, rows2],
        out_shape=[
            jax.ShapeDtypeStruct((1, ROWS, COLS), bf16),
            jax.ShapeDtypeStruct((RANK, COLS), f32),
            jax.ShapeDtypeStruct((ROWS, COLS), f32),
            jax.ShapeDtypeStruct((ROWS, COLS), bf16),
            jax.ShapeDtypeStruct((ROWS, COLS), bf16),
        ],
        scratch_shapes=[pltpu.VMEM((6 * RANK, COLS), bf16)],
        name="final",
    )(grads, errors, factor, sums, weight, first, second)


def exchange(x, axis):
    return lax.all_to_all(x, axis, 0, 0)


def shards(grads, errors, q_prev, weight, first_moment, second_moment):
    local = left_factor(grads, errors, q_prev).reshape(N_REP, 16, LANES)
    factor = exchange(sum_copies(exchange(local, "rep"), N_REP), "rep")
    factor = factor.reshape(ROWS // LANES, RANK, LANES)
    right = exchange(right_term(grads, errors, factor), "rep")
    right = exchange(sum_copies(right, N_FSDP), "fsdp")
    sums = exchange(sum_copies(right, N_REP), "rep")
    outs = final(grads, errors, factor, sums, weight, first_moment, second_moment)
    return outs[0], outs[1].T, *outs[2:]


def solution(mesh):
    return jax.shard_map(
        shards,
        mesh=mesh,
        in_specs=(
            P("rep", "fsdp", None),
            P("rep", "fsdp", None),
            P(),
            P("fsdp", None),
            P("fsdp", None),
            P("fsdp", None),
        ),
        out_specs=(P("rep", "fsdp", None), P(), P("fsdp", None), P("fsdp", None), P("fsdp", None)),
        check_vma=False,
    )
```

```python
import functools

import jax
import jax.numpy as jnp
from jax import lax
from jax.experimental import pallas as pl
from jax.experimental.pallas import tpu as pltpu
from jax.sharding import PartitionSpec as P

beta_first = 0.9
beta_second = 0.95
learn_rate = 0.05
weight_decay = 0.1
epsilon = 1e-08
correct_first = 1.0 - 0.9**10
correct_second = 1.0 - 0.95**10

ROWS, COLS, RANK, N_REP, N_FSDP = 1024, 512, 64, 32, 8
HALF, N_CHIP, PIECE = ROWS // 2, N_REP // 2, 16
LANES = 128
f32, bf16 = jnp.float32, jnp.bfloat16
NT = (((1,), (1,)), ((), ()))
NN = (((1,), (0,)), ((), ()))
TN = (((0,), (0,)), ((), ()))


def mm(a, b, dims):
    return lax.dot_general(a, b, dims, preferred_element_type=f32)


def split3(x):
    hi = x.astype(bf16)
    rest = x - hi.astype(f32)
    mid = rest.astype(bf16)
    lo = (rest - mid.astype(f32)).astype(bf16)
    return hi, mid, lo


def stack3(x):
    return jnp.concatenate(split3(x), axis=0)


def fold3(x):
    n = x.shape[0] // 3
    return x[:n] + x[n : 2 * n] + x[2 * n :]


def exact(a, b, dims):
    a1, a2, a3 = split3(a)
    b1, b2, b3 = split3(b)
    small = mm(a1, b3, dims) + mm(a3, b1, dims) + mm(a2, b2, dims)
    return small + (mm(a1, b2, dims) + mm(a2, b1, dims)) + mm(a1, b1, dims)


SMEM = pl.BlockSpec(memory_space=pltpu.SMEM)
VMEM = pl.BlockSpec(memory_space=pltpu.VMEM)
ANY = pl.BlockSpec(memory_space=pl.ANY)


def call(body, name, ins, outs, limit, scratch=(), cost=0):
    return pl.pallas_call(
        body,
        in_specs=ins,
        out_specs=[VMEM if m is None else m for _, _, m in outs],
        out_shape=[
            pltpu.VMEM(s, t) if m is None else jax.ShapeDtypeStruct(s, t) for s, t, m in outs
        ],
        scratch_shapes=scratch,
        compiler_params=pltpu.CompilerParams(vmem_limit_bytes=limit << 20),
        cost_estimate=pl.CostEstimate(flops=cost, bytes_accessed=cost // 64, transcendentals=0),
        name=name,
    )


def tile_columns(block, out):
    for k in range(out.shape[0]):
        out[k] = block[:, k * LANES : (k + 1) * LANES]


def left_first_body(core, grads, errors, q_prev, other, g_all, e_all, q_parts, q_buf, sems, q_sem):
    mine, theirs = core[0], 1 - core[0]
    q_copy = pltpu.make_async_copy(q_prev, q_buf, q_sem)
    copies = []
    for n, half in enumerate((theirs, mine)):
        rows = pl.ds(pl.multiple_of(half * HALF, HALF), HALF)
        copies.append(pltpu.make_async_copy(grads.at[0, rows], g_all.at[rows], sems.at[2 * n]))
        copies.append(pltpu.make_async_copy(errors.at[0, rows], e_all.at[rows], sems.at[2 * n + 1]))
    copies[0].start()
    copies[1].start()
    q_copy.start()
    copies[2].start()
    copies[3].start()
    q_copy.wait()
    q_parts[...] = stack3(q_buf[...])
    copies[0].wait()
    copies[1].wait()
    rows = pl.ds(pl.multiple_of(theirs * HALF, HALF), HALF)
    tile_columns(fold3(mm(q_parts[...], g_all[rows], NT) + mm(q_parts[...], e_all[rows], NT)), other)
    copies[2].wait()
    copies[3].wait()


def in_hbm(x):
    return pltpu.with_memory_space_constraint(x, pltpu.HBM)


def left_first(core, grads, errors, q_prev):
    return call(
        left_first_body, "left_first", [SMEM, ANY, ANY, ANY],
        [
            ((HALF // LANES, RANK, LANES), f32, None),
            ((ROWS, COLS), bf16, None),
            ((ROWS, COLS), bf16, None),
            ((3 * RANK, COLS), bf16, None),
        ],
        16,
        [pltpu.VMEM((RANK, COLS), f32), pltpu.SemaphoreType.DMA((4,)), pltpu.SemaphoreType.DMA],
        cost=200_000_000,
    )(core, in_hbm(grads), in_hbm(errors), in_hbm(q_prev.T))


def left_own_body(core, g_all, e_all, q_parts, out):
    rows = pl.ds(pl.multiple_of(core[0] * HALF, HALF), HALF)
    tile_columns(fold3(mm(q_parts[...], g_all[rows], NT) + mm(q_parts[...], e_all[rows], NT)), out)


def left_own(core, g_all, e_all, q_parts):
    return call(
        left_own_body, "left_own", [SMEM, VMEM, VMEM, VMEM],
        [((HALF // LANES, RANK, LANES), f32, None)], 8, cost=200_000_000,
    )(core, g_all, e_all, q_parts)[0]


def add_body(a, b, out):
    out[...] = a[...] + b[...]


def add(a, b):
    return call(add_body, "add", [VMEM, VMEM], [(a.shape, f32, None)], 4)(a, b)[0]


def sum_copies_body(pieces, out):
    total = pieces[0]
    for k in range(1, pieces.shape[0]):
        total = total + pieces[k]
    for k in range(out.shape[0]):
        out[k] = total


def sum_copies(pieces, copies):
    shape = (copies, *pieces.shape[1:])
    return call(sum_copies_body, "sum_copies", [VMEM], [(shape, f32, None)], 4)(pieces)[0]


def factor_parts(factor):
    return stack3(jnp.concatenate([factor[k] for k in range(factor.shape[0])], axis=1))


def square_of(parts):
    square = fold3(mm(parts, parts, NT))
    return square[:, :RANK] + square[:, RANK : 2 * RANK] + square[:, 2 * RANK :]


def right_first_body(core, g_all, e_all, factor, right, gram):
    rows = pl.ds(pl.multiple_of(core[0] * HALF, HALF), HALF)
    parts = factor_parts(factor)
    right[...] = fold3(mm(parts, g_all[rows], NN) + mm(parts, e_all[rows], NN))
    gram[...] = square_of(parts)


def right_first(core, g_all, e_all, factor):
    return call(
        right_first_body, "right_first", [SMEM, VMEM, VMEM, VMEM],
        [((RANK, COLS), f32, None), ((RANK, RANK), f32, None)], 8, cost=200_000_000,
    )(core, g_all, e_all, factor)


def half_tiles(block, out):
    for c in range(N_CHIP):
        i, j = divmod(c, COLS // 2 // LANES)
        out[c, :8] = block[8 * i : 8 * i + 8, LANES * j : LANES * (j + 1)]


def right_half(core, flip, g_all, e_all, parts, first):
    rows = pl.ds(pl.multiple_of((1 - core[0]) * HALF, HALF), HALF)
    half = core[0] if not flip else 1 - core[0]
    columns = pl.ds(pl.multiple_of(half * (COLS // 2), COLS // 2), COLS // 2)
    block = fold3(mm(parts, g_all[rows, columns], NN) + mm(parts, e_all[rows, columns], NN))
    return first[:, columns] + block


def right_theirs_body(core, g_all, e_all, factor, first, out):
    block = right_half(core, True, g_all, e_all, factor_parts(factor), first)
    for c in range(N_CHIP):
        i, j = divmod(c, COLS // 2 // LANES)
        out[c] = block[8 * i : 8 * i + 8, LANES * j : LANES * (j + 1)]


def right_theirs(core, g_all, e_all, factor, first):
    return call(
        right_theirs_body, "right_theirs", [SMEM, VMEM, VMEM, VMEM, VMEM],
        [((N_CHIP, 8, LANES), f32, None)], 8, cost=100_000_000,
    )(core, g_all, e_all, factor, first)[0]


def right_own_body(core, g_all, e_all, factor, first, gram, out):
    parts = factor_parts(factor)
    block = right_half(core, False, g_all, e_all, parts, first)
    square = (gram[...] + square_of(parts)) * (1.0 / N_CHIP)
    for c in range(N_CHIP):
        i, j = divmod(c, COLS // 2 // LANES)
        out[c, :8] = block[8 * i : 8 * i + 8, LANES * j : LANES * (j + 1)]
        out[c, 8:] = jnp.zeros((8, LANES), f32)
    for c in range(RANK // 8):
        out[c, 8:, :RANK] = square[8 * c : 8 * c + 8, :]


def right_own(core, g_all, e_all, factor, first, gram):
    return call(
        right_own_body, "right_own", [SMEM, VMEM, VMEM, VMEM, VMEM, VMEM],
        [((N_CHIP, PIECE, LANES), f32, None)], 8, cost=100_000_000,
    )(core, g_all, e_all, factor, first, gram)[0]


def right_join_body(own, arrived, out):
    out[:, :8] = own[:, :8] + arrived[...]
    out[:, 8:] = own[:, 8:]


def right_join(own, arrived):
    return call(
        right_join_body, "right_join", [VMEM, VMEM], [(own.shape, f32, None)], 4
    )(own, arrived)[0]


def inverse_triangle(gram):
    eye = (
        lax.broadcasted_iota(jnp.int32, (RANK, RANK), 0)
        == lax.broadcasted_iota(jnp.int32, (RANK, RANK), 1)
    ).astype(f32)
    both = jnp.concatenate([gram, eye], axis=1)
    groups = RANK // 8
    rows = [both[8 * g : 8 * g + 8] for g in range(groups)]
    tile = (8, 2 * RANK)
    sub = lax.broadcasted_iota(jnp.int32, tile, 0)
    done = []
    for b in range(groups):
        columns = [
            [
                jnp.broadcast_to(rows[g][:, 8 * b + j : 8 * b + j + 1], tile)
                for g in range(b, groups)
            ]
            for j in range(8)
        ]
        roots = jnp.zeros(tile, f32)
        for k in range(8):
            pivot = jnp.broadcast_to(columns[k][0][k : k + 1], tile)
            inv = 1.0 / pivot
            roots = jnp.where(sub == k, lax.rsqrt(pivot), roots)
            scale = [c * inv for c in columns[k]]
            scale[0] = jnp.where(sub > k, scale[0], 0.0)
            for j in range(k + 1, 8):
                head = jnp.broadcast_to(columns[j][0][k : k + 1], tile)
                columns[j] = [c - x * head for c, x in zip(columns[j], scale)]
            row = jnp.broadcast_to(rows[b][k : k + 1], tile)
            for g in range(b, groups):
                rows[g] = rows[g] - scale[g - b] * row
        done.append(rows[b] * roots)
    return jnp.concatenate(done, axis=0)[:, RANK:]


def solve_body(sums, inverse):
    gram = jnp.concatenate([sums[c, 8:, :RANK] for c in range(RANK // 8)], axis=0)
    inverse[...] = inverse_triangle(gram)


def solve(sums):
    return call(
        solve_body, "solve", [VMEM], [((RANK, RANK), f32, None)], 4, cost=4_000_000_000
    )(sums)[0]


STEP = 128


def final_body(
    core, grads, errors, factor_own, factor_other, sums_own, sums_other, inverse, weight, first, second,
    new_errors, q_next, new_weight, new_first, new_second,
    right, mix, factor, err_buf, weight_buf, first_buf, second_buf, sems,
):
    half = COLS // 2
    for source, place in ((sums_own, core[0]), (sums_other, 1 - core[0])):
        block = jnp.concatenate(
            [
                jnp.concatenate([source[2 * i, :8], source[2 * i + 1, :8]], axis=1)
                for i in range(RANK // 8)
            ],
            axis=0,
        )
        right[:, pl.ds(pl.multiple_of(place * half, half), half)] = block
    q_t = exact(inverse[...], right[...], NN) * (1.0 / N_REP)
    q_next[...] = q_t
    w1, w2, w3 = split3(exact(inverse[...], q_t, TN))
    mix[...] = jnp.concatenate([w1, w2, w1, w3, w2, w1], axis=0)
    tiles = HALF // LANES
    factor[pl.ds(core[0] * tiles, tiles)] = factor_own[...]
    factor[pl.ds((1 - core[0]) * tiles, tiles)] = factor_other[...]

    copies = []
    for step in range(ROWS // STEP):
        rows = pl.ds(step * STEP, STEP)
        per = STEP // LANES
        piece = jnp.concatenate([factor[step * per + k] for k in range(per)], axis=1)
        f1, f2, f3 = split3(piece)
        approx = mm(jnp.concatenate([f1, f1, f2, f1, f2, f3], axis=0), mix[...], TN)
        merged = grads[rows].astype(f32) + errors[rows].astype(f32)
        err_buf[rows] = (merged - approx).astype(bf16)
        first_f = beta_first * first[rows].astype(f32) + (1.0 - beta_first) * approx
        second_f = beta_second * second[rows].astype(f32) + ((1.0 - beta_second) * approx) * approx
        first_buf[rows] = first_f.astype(bf16)
        second_buf[rows] = second_f.astype(bf16)
        root = second_f * lax.rsqrt(second_f) * (1.0 / correct_second) ** 0.5 + epsilon
        ratio = (first_f * (learn_rate / correct_first)) / root
        weight_buf[rows] = weight[rows] * (1.0 - learn_rate * weight_decay) - ratio
        for n, (buf, out) in enumerate(
            (
                (err_buf, new_errors.at[0]),
                (weight_buf, new_weight),
                (first_buf, new_first),
                (second_buf, new_second),
            )
        ):
            copy = pltpu.make_async_copy(buf.at[rows], out.at[rows], sems.at[n, step])
            copy.start()
            copies.append(copy)
    for copy in copies:
        copy.wait()


def final(core, grads, errors, factor_own, factor_other, sums_own, sums_other, inverse, weight, first, second):
    wide = (ROWS, COLS)
    return call(
        final_body, "final", [SMEM] + [VMEM] * 10,
        [
            ((1, *wide), bf16, ANY),
            ((RANK, COLS), f32, VMEM),
            (wide, f32, ANY),
            (wide, bf16, ANY),
            (wide, bf16, ANY),
        ],
        16,
        [
            pltpu.VMEM((RANK, COLS), f32),
            pltpu.VMEM((6 * RANK, COLS), bf16),
            pltpu.VMEM((ROWS // LANES, RANK, LANES), f32),
            pltpu.VMEM(wide, bf16),
            pltpu.VMEM(wide, f32),
            pltpu.VMEM(wide, bf16),
            pltpu.VMEM(wide, bf16),
            pltpu.SemaphoreType.DMA((4, ROWS // STEP)),
        ],
        cost=400_000_000,
    )(core, grads, errors, factor_own, factor_other, sums_own, sums_other, inverse, weight, first, second)


PLANE = [[2 * p + c for p in range(N_CHIP)] for c in range(2)]
SWAP = [(i, i ^ 1) for i in range(N_REP)]


def exchange(x):
    return lax.all_to_all(x, "rep", 0, 0, axis_index_groups=PLANE)


def swap(x):
    return lax.ppermute(x, "rep", SWAP)


def shards(grads, errors, q_prev, weight, first_moment, second_moment):
    core = (lax.axis_index("rep") % 2).astype(jnp.int32).reshape(1)
    theirs, g_all, e_all, q_parts = left_first(core, grads, errors, q_prev)
    arrived = swap(theirs)
    own = left_own(core, g_all, e_all, q_parts)
    pieces = add(own, arrived).reshape(N_CHIP, PIECE, LANES)
    factor_own = exchange(sum_copies(exchange(pieces), N_CHIP)).reshape(own.shape)
    factor_other = swap(factor_own)
    first, gram = right_first(core, g_all, e_all, factor_own)
    arrived = swap(right_theirs(core, g_all, e_all, factor_other, first))
    own = right_own(core, g_all, e_all, factor_other, first, gram)
    pieces = sum_copies(exchange(right_join(own, arrived)), N_FSDP)
    pieces = sum_copies(lax.all_to_all(pieces, "fsdp", 0, 0), N_CHIP)
    sums_own = exchange(pieces)
    sums_other = swap(sums_own)
    inverse = solve(sums_own)
    outs = final(
        core, g_all, e_all, factor_own, factor_other, sums_own, sums_other, inverse,
        weight, first_moment, second_moment,
    )
    return outs[0], outs[1].T, *outs[2:]


def solution(mesh):
    return jax.shard_map(
        shards,
        mesh=mesh,
        in_specs=(
            P("rep", "fsdp", None),
            P("rep", "fsdp", None),
            P(),
            P("fsdp", None),
            P("fsdp", None),
            P("fsdp", None),
        ),
        out_specs=(P("rep", "fsdp", None), P(), P("fsdp", None), P("fsdp", None), P("fsdp", None)),
        check_vma=False,
    )
```

```python
import functools

import jax
import jax.numpy as jnp
from jax import lax
from jax.experimental import pallas as pl
from jax.experimental.pallas import tpu as pltpu
from jax.sharding import PartitionSpec as P

beta_first = 0.9
beta_second = 0.95
learn_rate = 0.05
weight_decay = 0.1
epsilon = 1e-08
correct_first = 1.0 - 0.9**10
correct_second = 1.0 - 0.95**10

ROWS, COLS, RANK, N_REP, N_FSDP = 1024, 512, 64, 32, 8
HALF, N_CHIP, OWN = ROWS // 2, N_REP // 2, ROWS // N_REP
LANES = 128
f32, bf16 = jnp.float32, jnp.bfloat16
NT = (((1,), (1,)), ((), ()))
NN = (((1,), (0,)), ((), ()))
TN = (((0,), (0,)), ((), ()))


def mm(a, b, dims):
    return lax.dot_general(a, b, dims, preferred_element_type=f32)


def split3(x):
    hi = x.astype(bf16)
    rest = x - hi.astype(f32)
    mid = rest.astype(bf16)
    lo = (rest - mid.astype(f32)).astype(bf16)
    return hi, mid, lo


def stack3(x):
    return jnp.concatenate(split3(x), axis=0)


def fold3(x):
    n = x.shape[0] // 3
    return x[:n] + x[n : 2 * n] + x[2 * n :]


def exact(a, b, dims):
    a1, a2, a3 = split3(a)
    b1, b2, b3 = split3(b)
    small = mm(a1, b3, dims) + mm(a3, b1, dims) + mm(a2, b2, dims)
    return small + (mm(a1, b2, dims) + mm(a2, b1, dims)) + mm(a1, b1, dims)


SMEM = pl.BlockSpec(memory_space=pltpu.SMEM)
VMEM = pl.BlockSpec(memory_space=pltpu.VMEM)
ANY = pl.BlockSpec(memory_space=pl.ANY)


def call(body, name, ins, outs, limit, scratch=(), cost=0):
    return pl.pallas_call(
        body,
        in_specs=ins,
        out_specs=[VMEM if m is None else m for _, _, m in outs],
        out_shape=[
            pltpu.VMEM(s, t) if m is None else jax.ShapeDtypeStruct(s, t) for s, t, m in outs
        ],
        scratch_shapes=scratch,
        compiler_params=pltpu.CompilerParams(vmem_limit_bytes=limit << 20),
        cost_estimate=pl.CostEstimate(flops=cost, bytes_accessed=cost // 64, transcendentals=0),
        name=name,
    )


def tile_columns(block, out):
    for k in range(out.shape[0]):
        out[k] = block[:, k * LANES : (k + 1) * LANES]


def merge_body(flip, core, grads, errors, merged, g_half, e_half, sems):
    half = 1 - core[0] if flip else core[0]
    rows = pl.ds(pl.multiple_of(half * HALF, HALF), HALF)
    copies = [
        pltpu.make_async_copy(grads.at[0, rows], g_half, sems.at[0]),
        pltpu.make_async_copy(errors.at[0, rows], e_half, sems.at[1]),
    ]
    for copy in copies:
        copy.start()
    for copy in copies:
        copy.wait()
    merged[...] = g_half[...].astype(f32) + e_half[...].astype(f32)


def in_hbm(x):
    return pltpu.with_memory_space_constraint(x, pltpu.HBM)


def merge_half(flip, core, grads, errors):
    half = (HALF, COLS)
    return call(
        functools.partial(merge_body, flip), "merge_theirs" if flip else "merge_own",
        [SMEM, ANY, ANY], [(half, f32, None), (half, bf16, None), (half, bf16, None)],
        16, [pltpu.SemaphoreType.DMA((2,))], cost=200_000_000,
    )(core, in_hbm(grads), in_hbm(errors))


def add_body(a, b, out):
    out[...] = a[...] + b[...]


def add(a, b):
    return call(add_body, "add", [VMEM, VMEM], [(a.shape, f32, None)], 8)(a, b)[0]


def sum_copies_body(pieces, out):
    total = pieces[0]
    for k in range(1, pieces.shape[0]):
        total = total + pieces[k]
    for k in range(out.shape[0]):
        out[k] = total


def sum_copies(pieces, copies):
    shape = (copies, *pieces.shape[1:])
    return call(sum_copies_body, "sum_copies", [VMEM], [(shape, f32, None)], 4)(pieces)[0]


def terms_body(pieces, q_prev, factor, out, right):
    merged = pieces[0]
    for k in range(1, N_CHIP):
        merged = merged + pieces[k]
    m_parts = split3(merged)
    left = fold3(mm(jnp.concatenate(m_parts, axis=0), stack3(q_prev[...]), NT))
    left = left[:, :RANK] + left[:, RANK : 2 * RANK] + left[:, 2 * RANK :]
    factor[...] = jnp.concatenate([left[: OWN // 2], left[OWN // 2 :]], axis=1)
    parts = stack3(left.T)
    m1, m2, m3 = m_parts
    right[...] = fold3((mm(parts, m3, NN) + mm(parts, m2, NN)) + mm(parts, m1, NN))
    gram = fold3(mm(parts, parts, NT))
    gram = gram[:, :RANK] + gram[:, RANK : 2 * RANK] + gram[:, 2 * RANK :]
    per = COLS // 2 // LANES
    for r in range(N_REP):
        i, j = divmod(r // 2, per)
        column = LANES * (j + per * (r % 2))
        for k in range(4):
            out[r, k] = right[8 * i + 2 * k : 8 * i + 2 * k + 2, column : column + LANES]
    for p in range(N_CHIP):
        first, second = gram[4 * p : 4 * p + 2], gram[4 * p + 2 : 4 * p + 4]
        both = jnp.concatenate([first, second], axis=1)
        out[2 * p, 4] = both
        out[2 * p + 1, 4] = both


def terms(pieces, q_prev):
    return call(
        terms_body, "terms", [VMEM, VMEM],
        [((OWN // 2, LANES), f32, None), ((N_REP, 5, 2, LANES), f32, None)],
        16, [pltpu.VMEM((RANK, COLS), f32)], cost=100_000_000,
    )(pieces, q_prev.T)


def last_sum_body(pieces, factor, out):
    total = pieces[0]
    for k in range(1, N_FSDP):
        total = total + pieces[k]
    for k in range(N_CHIP):
        for n in range(5):
            out[k, 2 * n : 2 * n + 2] = total[n]
        out[k, 10:16] = jnp.zeros((6, LANES), f32)
        out[k, 16:] = factor[...]


def last_sum(pieces, factor):
    return call(
        last_sum_body, "last_sum", [VMEM, VMEM], [((N_CHIP, 32, LANES), f32, None)], 4
    )(pieces, factor)[0]


def inverse_triangle(gram):
    eye = (
        lax.broadcasted_iota(jnp.int32, (RANK, RANK), 0)
        == lax.broadcasted_iota(jnp.int32, (RANK, RANK), 1)
    ).astype(f32)
    both = jnp.concatenate([gram, eye], axis=1)
    groups = RANK // 8
    rows = [both[8 * g : 8 * g + 8] for g in range(groups)]
    tile = (8, 2 * RANK)
    sub = lax.broadcasted_iota(jnp.int32, tile, 0)
    done = []
    for b in range(groups):
        columns = [
            [
                jnp.broadcast_to(rows[g][:, 8 * b + j : 8 * b + j + 1], tile)
                for g in range(b, groups)
            ]
            for j in range(8)
        ]
        roots = jnp.zeros(tile, f32)
        for k in range(8):
            pivot = jnp.broadcast_to(columns[k][0][k : k + 1], tile)
            inv = 1.0 / pivot
            roots = jnp.where(sub == k, lax.rsqrt(pivot), roots)
            scale = [c * inv for c in columns[k]]
            scale[0] = jnp.where(sub > k, scale[0], 0.0)
            for j in range(k + 1, 8):
                head = jnp.broadcast_to(columns[j][0][k : k + 1], tile)
                columns[j] = [c - x * head for c, x in zip(columns[j], scale)]
            row = jnp.broadcast_to(rows[b][k : k + 1], tile)
            for g in range(b, groups):
                rows[g] = rows[g] - scale[g - b] * row
        done.append(rows[b] * roots)
    return jnp.concatenate(done, axis=0)[:, RANK:]


def solve_body(sums, inverse):
    gram = jnp.concatenate(
        [sums[p, 8:10, half : half + RANK] for p in range(N_CHIP) for half in (0, RANK)], axis=0
    )
    inverse[...] = inverse_triangle(gram)


def solve(sums):
    return call(
        solve_body, "solve", [VMEM], [((RANK, RANK), f32, None)], 4, cost=4_000_000_000
    )(sums)[0]


STEP = 128


def final_body(
    core, g_own, e_own, g_other, e_other, sums_own, sums_other, inverse, weight, first, second,
    new_errors, q_next, new_weight, new_first, new_second,
    right, mix, factor, err_buf, weight_buf, first_buf, second_buf, sems,
):
    half = COLS // 2
    for source, place in ((sums_own, core[0]), (sums_other, 1 - core[0])):
        block = jnp.concatenate(
            [
                jnp.concatenate([source[2 * i, :8], source[2 * i + 1, :8]], axis=1)
                for i in range(RANK // 8)
            ],
            axis=0,
        )
        right[:, pl.ds(pl.multiple_of(place * half, half), half)] = block
        for p in range(N_CHIP):
            n = OWN // 2
            at = pl.multiple_of(place * HALF + OWN * p, OWN)
            factor[pl.ds(at, n)] = source[p, 16:, :RANK]
            factor[pl.ds(at + n, n)] = source[p, 16:, RANK:]
    q_t = exact(inverse[...], right[...], NN) * (1.0 / N_REP)
    q_next[...] = q_t
    w1, w2, w3 = split3(exact(inverse[...], q_t, TN))
    mix[...] = jnp.concatenate([w1, w2, w1, w3, w2, w1], axis=0)

    copies = []
    for step in range(ROWS // STEP):
        other, n = divmod(step * STEP, HALF)
        place = 1 - core[0] if other else core[0]
        grads, errors = (g_other, e_other) if other else (g_own, e_own)
        piece = slice(n, n + STEP)
        rows = pl.ds(pl.multiple_of(place * HALF + n, STEP), STEP)
        f1, f2, f3 = (f.astype(f32) for f in split3(factor[rows]))
        pairs = ((f1, f1), (f2, f1), (f2, f3))
        wide = [jnp.concatenate(pair, axis=1).astype(bf16) for pair in pairs]
        approx = mm(jnp.concatenate(wide, axis=1), mix[...], NN)
        merged = grads[piece].astype(f32) + errors[piece].astype(f32)
        err_buf[rows] = (merged - approx).astype(bf16)
        first_f = beta_first * first[rows].astype(f32) + (1.0 - beta_first) * approx
        second_f = beta_second * second[rows].astype(f32) + ((1.0 - beta_second) * approx) * approx
        first_buf[rows] = first_f.astype(bf16)
        second_buf[rows] = second_f.astype(bf16)
        root = second_f * lax.rsqrt(second_f) * (1.0 / correct_second) ** 0.5 + epsilon
        ratio = (first_f * (learn_rate / correct_first)) / root
        weight_buf[rows] = weight[rows] * (1.0 - learn_rate * weight_decay) - ratio
        for n, (buf, out) in enumerate(
            (
                (err_buf, new_errors.at[0]),
                (weight_buf, new_weight),
                (first_buf, new_first),
                (second_buf, new_second),
            )
        ):
            copy = pltpu.make_async_copy(buf.at[rows], out.at[rows], sems.at[n, step])
            copy.start()
            copies.append(copy)
    for copy in copies:
        copy.wait()


def final(core, own, other, sums_own, sums_other, inverse, weight, first, second):
    wide = (ROWS, COLS)
    return call(
        final_body, "final", [SMEM] + [VMEM] * 10,
        [
            ((1, *wide), bf16, ANY),
            ((RANK, COLS), f32, VMEM),
            (wide, f32, ANY),
            (wide, bf16, ANY),
            (wide, bf16, ANY),
        ],
        16,
        [
            pltpu.VMEM((RANK, COLS), f32),
            pltpu.VMEM((6 * RANK, COLS), bf16),
            pltpu.VMEM((ROWS, RANK), f32),
            pltpu.VMEM(wide, bf16),
            pltpu.VMEM(wide, f32),
            pltpu.VMEM(wide, bf16),
            pltpu.VMEM(wide, bf16),
            pltpu.SemaphoreType.DMA((4, ROWS // STEP)),
        ],
        cost=400_000_000,
    )(core, *own, *other, sums_own, sums_other, inverse, weight, first, second)


PLANE = [[2 * p + c for p in range(N_CHIP)] for c in range(2)]
SWAP = [(i, i ^ 1) for i in range(N_REP)]


def exchange(x):
    return lax.all_to_all(x, "rep", 0, 0, axis_index_groups=PLANE)


def swap(x):
    return lax.ppermute(x, "rep", SWAP)


def shards(grads, errors, q_prev, weight, first_moment, second_moment):
    core = (lax.axis_index("rep") % 2).astype(jnp.int32).reshape(1)
    theirs, *other = merge_half(True, core, grads, errors)
    arrived = swap(theirs)
    mine, *own = merge_half(False, core, grads, errors)
    pieces = exchange(add(mine, arrived).reshape(N_CHIP, OWN, COLS))
    factor, right = terms(pieces, q_prev)
    pieces = sum_copies(lax.all_to_all(right, "rep", 0, 0), N_FSDP)
    pieces = last_sum(lax.all_to_all(pieces, "fsdp", 0, 0), factor)
    sums_own = exchange(pieces)
    sums_other = swap(sums_own)
    inverse = solve(sums_own)
    outs = final(
        core, own, other, sums_own, sums_other, inverse, weight, first_moment, second_moment
    )
    return outs[0], outs[1].T, *outs[2:]


def solution(mesh):
    return jax.shard_map(
        shards,
        mesh=mesh,
        in_specs=(
            P("rep", "fsdp", None),
            P("rep", "fsdp", None),
            P(),
            P("fsdp", None),
            P("fsdp", None),
            P("fsdp", None),
        ),
        out_specs=(P("rep", "fsdp", None), P(), P("fsdp", None), P("fsdp", None), P("fsdp", None)),
        check_vma=False,
    )
```

```python
import functools

import jax
import jax.numpy as jnp
from jax import lax
from jax.experimental import pallas as pl
from jax.experimental.pallas import tpu as pltpu
from jax.sharding import PartitionSpec as P

beta_first = 0.9
beta_second = 0.95
learn_rate = 0.05
weight_decay = 0.1
epsilon = 1e-08
correct_first = 1.0 - 0.9**10
correct_second = 1.0 - 0.95**10

ROWS, COLS, RANK, N_REP, N_FSDP = 1024, 512, 64, 32, 8
HALF, N_CHIP, OWN = ROWS // 2, N_REP // 2, ROWS // N_REP
LANES = 128
f32, bf16 = jnp.float32, jnp.bfloat16
NT = (((1,), (1,)), ((), ()))
NN = (((1,), (0,)), ((), ()))
TN = (((0,), (0,)), ((), ()))


def mm(a, b, dims):
    return lax.dot_general(a, b, dims, preferred_element_type=f32)


def split3(x):
    hi = x.astype(bf16)
    rest = x - hi.astype(f32)
    mid = rest.astype(bf16)
    lo = (rest - mid.astype(f32)).astype(bf16)
    return hi, mid, lo


def stack3(x):
    return jnp.concatenate(split3(x), axis=0)


def fold3(x):
    n = x.shape[0] // 3
    return x[:n] + x[n : 2 * n] + x[2 * n :]


def exact(a, b, dims):
    a1, a2, a3 = split3(a)
    b1, b2, b3 = split3(b)
    small = mm(a1, b3, dims) + mm(a3, b1, dims) + mm(a2, b2, dims)
    return small + (mm(a1, b2, dims) + mm(a2, b1, dims)) + mm(a1, b1, dims)


SMEM = pl.BlockSpec(memory_space=pltpu.SMEM)
VMEM = pl.BlockSpec(memory_space=pltpu.VMEM)
ANY = pl.BlockSpec(memory_space=pl.ANY)


def call(body, name, ins, outs, limit, scratch=(), cost=0):
    return pl.pallas_call(
        body,
        in_specs=ins,
        out_specs=[VMEM if m is None else m for _, _, m in outs],
        out_shape=[
            pltpu.VMEM(s, t) if m is None else jax.ShapeDtypeStruct(s, t) for s, t, m in outs
        ],
        scratch_shapes=scratch,
        compiler_params=pltpu.CompilerParams(vmem_limit_bytes=limit << 20),
        cost_estimate=pl.CostEstimate(flops=cost, bytes_accessed=cost // 64, transcendentals=0),
        name=name,
    )


def tile_columns(block, out):
    for k in range(out.shape[0]):
        out[k] = block[:, k * LANES : (k + 1) * LANES]


def merge_body(flip, core, grads, errors, *refs):
    if flip:
        merged, g_half, e_half, sems = refs
        copies = []
    else:
        weight, merged, g_half, e_half, weight_kept, sems = refs
        copies = [pltpu.make_async_copy(weight, weight_kept, sems.at[2])]
    half = 1 - core[0] if flip else core[0]
    rows = pl.ds(pl.multiple_of(half * HALF, HALF), HALF)
    pair = [
        pltpu.make_async_copy(grads.at[0, rows], g_half, sems.at[0]),
        pltpu.make_async_copy(errors.at[0, rows], e_half, sems.at[1]),
    ]
    for copy in pair + copies:
        copy.start()
    for copy in pair:
        copy.wait()
    merged[...] = g_half[...].astype(f32) + e_half[...].astype(f32)
    for copy in copies:
        copy.wait()


def in_hbm(x):
    return pltpu.with_memory_space_constraint(x, pltpu.HBM)


def merge_half(flip, core, *arrays):
    half = (HALF, COLS)
    outs = [(half, f32, None), (half, bf16, None), (half, bf16, None)]
    if not flip:
        outs.append(((ROWS, COLS), f32, None))
    return call(
        functools.partial(merge_body, flip), "merge_theirs" if flip else "merge_own",
        [SMEM] + [ANY] * len(arrays), outs,
        16, [pltpu.SemaphoreType.DMA((3,))], cost=200_000_000,
    )(core, *(in_hbm(x) for x in arrays))


def add_body(a, b, out):
    out[...] = a[...] + b[...]


def add(a, b):
    return call(add_body, "add", [VMEM, VMEM], [(a.shape, f32, None)], 8)(a, b)[0]


def sum_copies_body(pieces, out):
    total = pieces[0]
    for k in range(1, pieces.shape[0]):
        total = total + pieces[k]
    for k in range(out.shape[0]):
        out[k] = total


def sum_copies(pieces, copies):
    shape = (copies, *pieces.shape[1:])
    return call(sum_copies_body, "sum_copies", [VMEM], [(shape, f32, None)], 4)(pieces)[0]


def terms_body(pieces, q_prev, factor, out, right):
    merged = pieces[0]
    for k in range(1, N_CHIP):
        merged = merged + pieces[k]
    m_parts = split3(merged)
    left = fold3(mm(jnp.concatenate(m_parts, axis=0), stack3(q_prev[...]), NT))
    left = left[:, :RANK] + left[:, RANK : 2 * RANK] + left[:, 2 * RANK :]
    factor[...] = jnp.concatenate([left[: OWN // 2], left[OWN // 2 :]], axis=1)
    parts = stack3(left.T)
    m1, m2, m3 = m_parts
    right[...] = fold3((mm(parts, m3, NN) + mm(parts, m2, NN)) + mm(parts, m1, NN))
    gram = fold3(mm(parts, parts, NT))
    gram = gram[:, :RANK] + gram[:, RANK : 2 * RANK] + gram[:, 2 * RANK :]
    per = COLS // 2 // LANES
    for r in range(N_REP):
        i, j = divmod(r // 2, per)
        column = LANES * (j + per * (r % 2))
        for k in range(4):
            out[r, k] = right[8 * i + 2 * k : 8 * i + 2 * k + 2, column : column + LANES]
    for p in range(N_CHIP):
        first, second = gram[4 * p : 4 * p + 2], gram[4 * p + 2 : 4 * p + 4]
        both = jnp.concatenate([first, second], axis=1)
        out[2 * p, 4] = both
        out[2 * p + 1, 4] = both


def terms(pieces, q_prev):
    return call(
        terms_body, "terms", [VMEM, VMEM],
        [((OWN // 2, LANES), f32, None), ((N_REP, 5, 2, LANES), f32, None)],
        16, [pltpu.VMEM((RANK, COLS), f32)], cost=100_000_000,
    )(pieces, q_prev.T)


def last_sum_body(pieces, factor, out):
    total = pieces[0]
    for k in range(1, N_FSDP):
        total = total + pieces[k]
    for k in range(N_CHIP):
        for n in range(5):
            out[k, 2 * n : 2 * n + 2] = total[n]
        out[k, 10:16] = jnp.zeros((6, LANES), f32)
        out[k, 16:] = factor[...]


def last_sum(pieces, factor):
    return call(
        last_sum_body, "last_sum", [VMEM, VMEM], [((N_CHIP, 32, LANES), f32, None)], 4
    )(pieces, factor)[0]


PANEL = 16


def inverse_triangle(gram):
    eye = (
        lax.broadcasted_iota(jnp.int32, (RANK, RANK), 0)
        == lax.broadcasted_iota(jnp.int32, (RANK, RANK), 1)
    ).astype(f32)
    both = jnp.concatenate([gram, eye], axis=1)
    groups = RANK // 8
    rows = [both[8 * g : 8 * g + 8] for g in range(groups)]
    tile = (8, 2 * RANK)
    sub = lax.broadcasted_iota(jnp.int32, tile, 0)
    pivots = [jnp.ones(tile, f32)] * groups
    for start in range(0, RANK, PANEL):
        columns = [
            {
                g: jnp.broadcast_to(rows[g][:, start + j : start + j + 1], tile)
                for g in range(start // 8, groups)
            }
            for j in range(PANEL)
        ]
        for k in range(PANEL):
            at, line = divmod(start + k, 8)
            pivot = jnp.broadcast_to(columns[k][at][line : line + 1], tile)
            inv = 1.0 / pivot
            pivots[at] = jnp.where(sub == line, pivot, pivots[at])
            scale = {g: c * inv for g, c in columns[k].items() if g >= at}
            scale[at] = jnp.where(sub > line, scale[at], 0.0)
            for j in range(k + 1, PANEL):
                head = jnp.broadcast_to(columns[j][at][line : line + 1], tile)
                for g in scale:
                    columns[j][g] = columns[j][g] - scale[g] * head
            row = jnp.broadcast_to(rows[at][line : line + 1], tile)
            for g in scale:
                rows[g] = rows[g] - scale[g] * row
    done = [row * lax.rsqrt(pivot) for row, pivot in zip(rows, pivots)]
    return jnp.concatenate(done, axis=0)[:, RANK:]


def solve_body(sums, inverse):
    gram = jnp.concatenate(
        [sums[p, 8:10, half : half + RANK] for p in range(N_CHIP) for half in (0, RANK)], axis=0
    )
    inverse[...] = inverse_triangle(gram)


def solve(sums):
    return call(
        solve_body, "solve", [VMEM], [((RANK, RANK), f32, None)], 4, cost=4_000_000_000
    )(sums)[0]


STEP = 128


def final_body(
    core, g_own, e_own, g_other, e_other, sums_own, sums_other, inverse, weight, first, second,
    new_errors, q_next, new_weight, new_first, new_second,
    right, mix, factor, err_buf, weight_buf, first_buf, second_buf, sems,
):
    half = COLS // 2
    for source, place in ((sums_own, core[0]), (sums_other, 1 - core[0])):
        block = jnp.concatenate(
            [
                jnp.concatenate([source[2 * i, :8], source[2 * i + 1, :8]], axis=1)
                for i in range(RANK // 8)
            ],
            axis=0,
        )
        right[:, pl.ds(pl.multiple_of(place * half, half), half)] = block
        for p in range(N_CHIP):
            n = OWN // 2
            at = pl.multiple_of(place * HALF + OWN * p, OWN)
            factor[pl.ds(at, n)] = source[p, 16:, :RANK]
            factor[pl.ds(at + n, n)] = source[p, 16:, RANK:]
    q_t = exact(inverse[...], right[...], NN) * (1.0 / N_REP)
    q_next[...] = q_t
    w1, w2, w3 = split3(exact(inverse[...], q_t, TN))
    mix[...] = jnp.concatenate([w1, w2, w1, w3, w2, w1], axis=0)

    copies = []
    for step in range(ROWS // STEP):
        other, n = divmod(step * STEP, HALF)
        place = 1 - core[0] if other else core[0]
        grads, errors = (g_other, e_other) if other else (g_own, e_own)
        piece = slice(n, n + STEP)
        rows = pl.ds(pl.multiple_of(place * HALF + n, STEP), STEP)
        f1, f2, f3 = (f.astype(f32) for f in split3(factor[rows]))
        pairs = ((f1, f1), (f2, f1), (f2, f3))
        wide = [jnp.concatenate(pair, axis=1).astype(bf16) for pair in pairs]
        approx = mm(jnp.concatenate(wide, axis=1), mix[...], NN)
        merged = grads[piece].astype(f32) + errors[piece].astype(f32)
        err_buf[rows] = (merged - approx).astype(bf16)
        first_f = beta_first * first[rows].astype(f32) + (1.0 - beta_first) * approx
        second_f = beta_second * second[rows].astype(f32) + ((1.0 - beta_second) * approx) * approx
        first_buf[rows] = first_f.astype(bf16)
        second_buf[rows] = second_f.astype(bf16)
        root = second_f * lax.rsqrt(second_f) * (1.0 / correct_second) ** 0.5 + epsilon
        ratio = (first_f * (learn_rate / correct_first)) / root
        weight_buf[rows] = weight[rows] * (1.0 - learn_rate * weight_decay) - ratio
        for n, (buf, out) in enumerate(
            (
                (err_buf, new_errors.at[0]),
                (weight_buf, new_weight),
                (first_buf, new_first),
                (second_buf, new_second),
            )
        ):
            copy = pltpu.make_async_copy(buf.at[rows], out.at[rows], sems.at[n, step])
            copy.start()
            copies.append(copy)
    for copy in copies:
        copy.wait()


def final(core, own, other, sums_own, sums_other, inverse, weight, first, second):
    wide = (ROWS, COLS)
    return call(
        final_body, "final", [SMEM] + [VMEM] * 10,
        [
            ((1, *wide), bf16, ANY),
            ((RANK, COLS), f32, VMEM),
            (wide, f32, ANY),
            (wide, bf16, ANY),
            (wide, bf16, ANY),
        ],
        16,
        [
            pltpu.VMEM((RANK, COLS), f32),
            pltpu.VMEM((6 * RANK, COLS), bf16),
            pltpu.VMEM((ROWS, RANK), f32),
            pltpu.VMEM(wide, bf16),
            pltpu.VMEM(wide, f32),
            pltpu.VMEM(wide, bf16),
            pltpu.VMEM(wide, bf16),
            pltpu.SemaphoreType.DMA((4, ROWS // STEP)),
        ],
        cost=400_000_000,
    )(core, *own, *other, sums_own, sums_other, inverse, weight, first, second)


PLANE = [[2 * p + c for p in range(N_CHIP)] for c in range(2)]
SWAP = [(i, i ^ 1) for i in range(N_REP)]


def exchange(x):
    return lax.all_to_all(x, "rep", 0, 0, axis_index_groups=PLANE)


def swap(x):
    return lax.ppermute(x, "rep", SWAP)


def shards(grads, errors, q_prev, weight, first_moment, second_moment):
    core = (lax.axis_index("rep") % 2).astype(jnp.int32).reshape(1)
    theirs, *other = merge_half(True, core, grads, errors)
    arrived = swap(theirs)
    mine, *own, weight = merge_half(False, core, grads, errors, weight)
    pieces = exchange(add(mine, arrived).reshape(N_CHIP, OWN, COLS))
    factor, right = terms(pieces, q_prev)
    pieces = sum_copies(lax.all_to_all(right, "rep", 0, 0), N_FSDP)
    pieces = last_sum(lax.all_to_all(pieces, "fsdp", 0, 0), factor)
    sums_own = exchange(pieces)
    sums_other = swap(sums_own)
    inverse = solve(sums_own)
    outs = final(
        core, own, other, sums_own, sums_other, inverse, weight, first_moment, second_moment
    )
    return outs[0], outs[1].T, *outs[2:]


def solution(mesh):
    return jax.shard_map(
        shards,
        mesh=mesh,
        in_specs=(
            P("rep", "fsdp", None),
            P("rep", "fsdp", None),
            P(),
            P("fsdp", None),
            P("fsdp", None),
            P("fsdp", None),
        ),
        out_specs=(P("rep", "fsdp", None), P(), P("fsdp", None), P("fsdp", None), P("fsdp", None)),
        check_vma=False,
    )
```

```python
import functools

import jax
import jax.numpy as jnp
from jax import lax
from jax.experimental import pallas as pl
from jax.experimental.pallas import tpu as pltpu
from jax.sharding import PartitionSpec as P

beta_first = 0.9
beta_second = 0.95
learn_rate = 0.05
weight_decay = 0.1
epsilon = 1e-08
correct_first = 1.0 - 0.9**10
correct_second = 1.0 - 0.95**10

ROWS, COLS, RANK, N_REP, N_FSDP = 1024, 512, 64, 32, 8
HALF, N_CHIP, OWN = ROWS // 2, N_REP // 2, ROWS // N_REP
LANES = 128
f32, bf16 = jnp.float32, jnp.bfloat16
NT = (((1,), (1,)), ((), ()))
NN = (((1,), (0,)), ((), ()))
TN = (((0,), (0,)), ((), ()))


def mm(a, b, dims):
    return lax.dot_general(a, b, dims, preferred_element_type=f32)


def split3(x):
    hi = x.astype(bf16)
    rest = x - hi.astype(f32)
    mid = rest.astype(bf16)
    lo = (rest - mid.astype(f32)).astype(bf16)
    return hi, mid, lo


def stack3(x):
    return jnp.concatenate(split3(x), axis=0)


def fold3(x):
    n = x.shape[0] // 3
    return x[:n] + x[n : 2 * n] + x[2 * n :]


def left_pieces(x):
    x1, x2, x3 = (p.astype(f32) for p in split3(x))
    pairs = ((x1, x1), (x2, x1), (x2, x3))
    return jnp.concatenate([jnp.concatenate(p, axis=1).astype(bf16) for p in pairs], axis=1)


def right_pieces(x):
    x1, x2, x3 = split3(x)
    return jnp.concatenate([x1, x2, x1, x3, x2, x1], axis=0)


SMEM = pl.BlockSpec(memory_space=pltpu.SMEM)
VMEM = pl.BlockSpec(memory_space=pltpu.VMEM)
ANY = pl.BlockSpec(memory_space=pl.ANY)


def call(body, name, ins, outs, limit, scratch=(), cost=0):
    return pl.pallas_call(
        body,
        in_specs=ins,
        out_specs=[VMEM if m is None else m for _, _, m in outs],
        out_shape=[
            pltpu.VMEM(s, t) if m is None else jax.ShapeDtypeStruct(s, t) for s, t, m in outs
        ],
        scratch_shapes=scratch,
        compiler_params=pltpu.CompilerParams(vmem_limit_bytes=limit << 20),
        cost_estimate=pl.CostEstimate(flops=cost, bytes_accessed=cost // 64, transcendentals=0),
        name=name,
    )


def merge_body(flip, core, grads, errors, *refs):
    if flip:
        merged, g_half, e_half, sems = refs
        copies = []
    else:
        weight, merged, g_half, e_half, weight_kept, sems = refs
        copies = [pltpu.make_async_copy(weight, weight_kept, sems.at[2])]
    half = 1 - core[0] if flip else core[0]
    rows = pl.ds(pl.multiple_of(half * HALF, HALF), HALF)
    pair = [
        pltpu.make_async_copy(grads.at[0, rows], g_half, sems.at[0]),
        pltpu.make_async_copy(errors.at[0, rows], e_half, sems.at[1]),
    ]
    for copy in pair + copies:
        copy.start()
    for copy in pair:
        copy.wait()
    merged[...] = g_half[...].astype(f32) + e_half[...].astype(f32)
    for copy in copies:
        copy.wait()


def in_hbm(x):
    return pltpu.with_memory_space_constraint(x, pltpu.HBM)


def merge_half(flip, core, *arrays):
    half = (HALF, COLS)
    outs = [(half, f32, None), (half, bf16, None), (half, bf16, None)]
    if not flip:
        outs.append(((ROWS, COLS), f32, None))
    return call(
        functools.partial(merge_body, flip), "merge_theirs" if flip else "merge_own",
        [SMEM] + [ANY] * len(arrays), outs,
        16, [pltpu.SemaphoreType.DMA((3,))], cost=200_000_000,
    )(core, *(in_hbm(x) for x in arrays))


def add_body(a, b, out):
    out[...] = a[...] + b[...]


def add(a, b):
    return call(add_body, "add", [VMEM, VMEM], [(a.shape, f32, None)], 8)(a, b)[0]


def sum_copies_body(pieces, out):
    total = pieces[0]
    for k in range(1, pieces.shape[0]):
        total = total + pieces[k]
    for k in range(out.shape[0]):
        out[k] = total


def sum_copies(pieces, copies):
    shape = (copies, *pieces.shape[1:])
    return call(sum_copies_body, "sum_copies", [VMEM], [(shape, f32, None)], 4)(pieces)[0]


def terms_body(pieces, q_prev, factor, out, right):
    merged = pieces[0]
    for k in range(1, N_CHIP):
        merged = merged + pieces[k]
    m_parts = split3(merged)
    left = fold3(mm(jnp.concatenate(m_parts, axis=0), stack3(q_prev[...]), NT))
    left = left[:, :RANK] + left[:, RANK : 2 * RANK] + left[:, 2 * RANK :]
    factor[...] = jnp.concatenate([left[: OWN // 2], left[OWN // 2 :]], axis=1)
    parts = stack3(left.T)
    m1, m2, m3 = m_parts
    right[...] = fold3((mm(parts, m3, NN) + mm(parts, m2, NN)) + mm(parts, m1, NN))
    gram = fold3(mm(parts, parts, NT))
    gram = gram[:, :RANK] + gram[:, RANK : 2 * RANK] + gram[:, 2 * RANK :]
    per = COLS // 2 // LANES
    for r in range(N_REP):
        i, j = divmod(r // 2, per)
        column = LANES * (j + per * (r % 2))
        for k in range(4):
            out[r, k] = right[8 * i + 2 * k : 8 * i + 2 * k + 2, column : column + LANES]
    for p in range(N_CHIP):
        first, second = gram[4 * p : 4 * p + 2], gram[4 * p + 2 : 4 * p + 4]
        both = jnp.concatenate([first, second], axis=1)
        out[2 * p, 4] = both
        out[2 * p + 1, 4] = both


def terms(pieces, q_prev):
    return call(
        terms_body, "terms", [VMEM, VMEM],
        [((OWN // 2, LANES), f32, None), ((N_REP, 5, 2, LANES), f32, None)],
        16, [pltpu.VMEM((RANK, COLS), f32)], cost=100_000_000,
    )(pieces, q_prev.T)


def last_sum_body(pieces, factor, out):
    total = pieces[0]
    for k in range(1, N_FSDP):
        total = total + pieces[k]
    for k in range(N_CHIP):
        for n in range(5):
            out[k, 2 * n : 2 * n + 2] = total[n]
        out[k, 10:16] = jnp.zeros((6, LANES), f32)
        out[k, 16:] = factor[...]


def last_sum(pieces, factor):
    return call(
        last_sum_body, "last_sum", [VMEM, VMEM], [((N_CHIP, 32, LANES), f32, None)], 4
    )(pieces, factor)[0]


PANEL = 16


def inverse_triangle(gram):
    eye = (
        lax.broadcasted_iota(jnp.int32, (RANK, RANK), 0)
        == lax.broadcasted_iota(jnp.int32, (RANK, RANK), 1)
    ).astype(f32)
    both = jnp.concatenate([gram, eye], axis=1)
    groups = RANK // 8
    rows = [both[8 * g : 8 * g + 8] for g in range(groups)]
    tile = (8, 2 * RANK)
    sub = lax.broadcasted_iota(jnp.int32, tile, 0)
    pivots = [jnp.ones(tile, f32)] * groups
    for start in range(0, RANK, PANEL):
        columns = [
            {
                g: jnp.broadcast_to(rows[g][:, start + j : start + j + 1], tile)
                for g in range(start // 8, groups)
            }
            for j in range(PANEL)
        ]
        for k in range(PANEL):
            at, line = divmod(start + k, 8)
            pivot = jnp.broadcast_to(columns[k][at][line : line + 1], tile)
            inv = 1.0 / pivot
            pivots[at] = jnp.where(sub == line, pivot, pivots[at])
            scale = {g: c * inv for g, c in columns[k].items() if g >= at}
            scale[at] = jnp.where(sub > line, scale[at], 0.0)
            for j in range(k + 1, PANEL):
                head = jnp.broadcast_to(columns[j][at][line : line + 1], tile)
                for g in scale:
                    columns[j][g] = columns[j][g] - scale[g] * head
            row = jnp.broadcast_to(rows[at][line : line + 1], tile)
            for g in scale:
                rows[g] = rows[g] - scale[g] * row
    done = [row * lax.rsqrt(pivot) for row, pivot in zip(rows, pivots)]
    return jnp.concatenate(done, axis=0)[:, RANK:]


def solve_body(sums, inverse):
    gram = jnp.concatenate(
        [sums[p, 8:10, half : half + RANK] for p in range(N_CHIP) for half in (0, RANK)], axis=0
    )
    inverse[...] = inverse_triangle(gram)


def solve(sums):
    return call(
        solve_body, "solve", [VMEM], [((RANK, RANK), f32, None)], 4, cost=4_000_000_000
    )(sums)[0]


STEP = 128


def final_body(
    core, g_own, e_own, g_other, e_other, sums_own, sums_other, inverse, weight, first, second,
    new_errors, q_next, new_weight, new_first, new_second,
    right, mix, factor, err_buf, weight_buf, first_buf, second_buf, sems,
):
    half = COLS // 2
    for source, place in ((sums_own, core[0]), (sums_other, 1 - core[0])):
        block = jnp.concatenate(
            [
                jnp.concatenate([source[2 * i, :8], source[2 * i + 1, :8]], axis=1)
                for i in range(RANK // 8)
            ],
            axis=0,
        )
        right[:, pl.ds(pl.multiple_of(place * half, half), half)] = block
        for p in range(N_CHIP):
            n = OWN // 2
            at = pl.multiple_of(place * HALF + OWN * p, OWN)
            factor[pl.ds(at, n)] = source[p, 16:, :RANK]
            factor[pl.ds(at + n, n)] = source[p, 16:, RANK:]
    q_t = mm(left_pieces(inverse[...]), right_pieces(right[...]), NN) * (1.0 / N_REP)
    q_next[...] = q_t
    mix[...] = right_pieces(mm(left_pieces(inverse[...].T), right_pieces(q_t), NN))

    copies = []
    for step in range(ROWS // STEP):
        other, n = divmod(step * STEP, HALF)
        place = 1 - core[0] if other else core[0]
        grads, errors = (g_other, e_other) if other else (g_own, e_own)
        piece = slice(n, n + STEP)
        rows = pl.ds(pl.multiple_of(place * HALF + n, STEP), STEP)
        approx = mm(left_pieces(factor[rows]), mix[...], NN)
        merged = grads[piece].astype(f32) + errors[piece].astype(f32)
        err_buf[rows] = (merged - approx).astype(bf16)
        first_f = beta_first * first[rows].astype(f32) + (1.0 - beta_first) * approx
        second_f = beta_second * second[rows].astype(f32) + ((1.0 - beta_second) * approx) * approx
        first_buf[rows] = first_f.astype(bf16)
        second_buf[rows] = second_f.astype(bf16)
        root = second_f * lax.rsqrt(second_f) * (1.0 / correct_second) ** 0.5 + epsilon
        ratio = (first_f * (learn_rate / correct_first)) / root
        weight_buf[rows] = weight[rows] * (1.0 - learn_rate * weight_decay) - ratio
        for n, (buf, out) in enumerate(
            (
                (err_buf, new_errors.at[0]),
                (weight_buf, new_weight),
                (first_buf, new_first),
                (second_buf, new_second),
            )
        ):
            copy = pltpu.make_async_copy(buf.at[rows], out.at[rows], sems.at[n, step])
            copy.start()
            copies.append(copy)
    for copy in copies:
        copy.wait()


def final(core, own, other, sums_own, sums_other, inverse, weight, first, second):
    wide = (ROWS, COLS)
    return call(
        final_body, "final", [SMEM] + [VMEM] * 10,
        [
            ((1, *wide), bf16, ANY),
            ((RANK, COLS), f32, VMEM),
            (wide, f32, ANY),
            (wide, bf16, ANY),
            (wide, bf16, ANY),
        ],
        16,
        [
            pltpu.VMEM((RANK, COLS), f32),
            pltpu.VMEM((6 * RANK, COLS), bf16),
            pltpu.VMEM((ROWS, RANK), f32),
            pltpu.VMEM(wide, bf16),
            pltpu.VMEM(wide, f32),
            pltpu.VMEM(wide, bf16),
            pltpu.VMEM(wide, bf16),
            pltpu.SemaphoreType.DMA((4, ROWS // STEP)),
        ],
        cost=400_000_000,
    )(core, *own, *other, sums_own, sums_other, inverse, weight, first, second)


PLANE = [[2 * p + c for p in range(N_CHIP)] for c in range(2)]
SWAP = [(i, i ^ 1) for i in range(N_REP)]


def exchange(x):
    return lax.all_to_all(x, "rep", 0, 0, axis_index_groups=PLANE)


def swap(x):
    return lax.ppermute(x, "rep", SWAP)


def shards(grads, errors, q_prev, weight, first_moment, second_moment):
    core = (lax.axis_index("rep") % 2).astype(jnp.int32).reshape(1)
    theirs, *other = merge_half(True, core, grads, errors)
    arrived = swap(theirs)
    mine, *own, weight = merge_half(False, core, grads, errors, weight)
    pieces = exchange(add(mine, arrived).reshape(N_CHIP, OWN, COLS))
    factor, right = terms(pieces, q_prev)
    pieces = sum_copies(lax.all_to_all(right, "rep", 0, 0), N_FSDP)
    pieces = last_sum(lax.all_to_all(pieces, "fsdp", 0, 0), factor)
    sums_own = exchange(pieces)
    sums_other = swap(sums_own)
    inverse = solve(sums_own)
    outs = final(
        core, own, other, sums_own, sums_other, inverse, weight, first_moment, second_moment
    )
    return outs[0], outs[1].T, *outs[2:]


def solution(mesh):
    return jax.shard_map(
        shards,
        mesh=mesh,
        in_specs=(
            P("rep", "fsdp", None),
            P("rep", "fsdp", None),
            P(),
            P("fsdp", None),
            P("fsdp", None),
            P("fsdp", None),
        ),
        out_specs=(P("rep", "fsdp", None), P(), P("fsdp", None), P("fsdp", None), P("fsdp", None)),
        check_vma=False,
    )
```

```python
import functools

import jax
import jax.numpy as jnp
from jax import lax
from jax.experimental import pallas as pl
from jax.experimental.pallas import tpu as pltpu
from jax.sharding import PartitionSpec as P

beta_first = 0.9
beta_second = 0.95
learn_rate = 0.05
weight_decay = 0.1
epsilon = 1e-08
correct_first = 1.0 - 0.9**10
correct_second = 1.0 - 0.95**10

ROWS, COLS, RANK, N_REP, N_FSDP = 1024, 512, 64, 32, 8
HALF, N_CHIP, OWN = ROWS // 2, N_REP // 2, ROWS // N_REP
LANES = 128
f32, bf16 = jnp.float32, jnp.bfloat16
NT = (((1,), (1,)), ((), ()))
NN = (((1,), (0,)), ((), ()))
TN = (((0,), (0,)), ((), ()))


def mm(a, b, dims):
    return lax.dot_general(a, b, dims, preferred_element_type=f32)


def split3(x):
    hi = x.astype(bf16)
    rest = x - hi.astype(f32)
    mid = rest.astype(bf16)
    lo = (rest - mid.astype(f32)).astype(bf16)
    return hi, mid, lo


def stack3(x):
    return jnp.concatenate(split3(x), axis=0)


def fold3(x):
    n = x.shape[0] // 3
    return x[:n] + x[n : 2 * n] + x[2 * n :]


def left_pieces(x):
    x1, x2, x3 = (p.astype(f32) for p in split3(x))
    pairs = ((x1, x1), (x2, x1), (x2, x3))
    return jnp.concatenate([jnp.concatenate(p, axis=1).astype(bf16) for p in pairs], axis=1)


def right_pieces(x):
    x1, x2, x3 = split3(x)
    return jnp.concatenate([x1, x2, x1, x3, x2, x1], axis=0)


SMEM = pl.BlockSpec(memory_space=pltpu.SMEM)
VMEM = pl.BlockSpec(memory_space=pltpu.VMEM)
ANY = pl.BlockSpec(memory_space=pl.ANY)


def call(body, name, ins, outs, limit, scratch=(), cost=0):
    return pl.pallas_call(
        body,
        in_specs=ins,
        out_specs=[VMEM if m is None else m for _, _, m in outs],
        out_shape=[
            pltpu.VMEM(s, t) if m is None else jax.ShapeDtypeStruct(s, t) for s, t, m in outs
        ],
        scratch_shapes=scratch,
        compiler_params=pltpu.CompilerParams(vmem_limit_bytes=limit << 20),
        cost_estimate=pl.CostEstimate(flops=cost, bytes_accessed=cost // 64, transcendentals=0),
        name=name,
    )


def merge_body(flip, core, grads, errors, *refs):
    if flip:
        merged, g_half, e_half, sems = refs
        copies = []
    else:
        weight, merged, g_half, e_half, weight_kept, sems = refs
        copies = [pltpu.make_async_copy(weight, weight_kept, sems.at[2])]
    half = 1 - core[0] if flip else core[0]
    rows = pl.ds(pl.multiple_of(half * HALF, HALF), HALF)
    pair = [
        pltpu.make_async_copy(grads.at[0, rows], g_half, sems.at[0]),
        pltpu.make_async_copy(errors.at[0, rows], e_half, sems.at[1]),
    ]
    for copy in pair + copies:
        copy.start()
    for copy in pair:
        copy.wait()
    merged[...] = g_half[...].astype(f32) + e_half[...].astype(f32)
    for copy in copies:
        copy.wait()


def in_hbm(x):
    return pltpu.with_memory_space_constraint(x, pltpu.HBM)


def merge_half(flip, core, *arrays):
    half = (HALF, COLS)
    outs = [(half, f32, None), (half, bf16, None), (half, bf16, None)]
    if not flip:
        outs.append(((ROWS, COLS), f32, None))
    return call(
        functools.partial(merge_body, flip), "merge_theirs" if flip else "merge_own",
        [SMEM] + [ANY] * len(arrays), outs,
        16, [pltpu.SemaphoreType.DMA((3,))], cost=200_000_000,
    )(core, *(in_hbm(x) for x in arrays))


def add_body(a, b, out):
    out[...] = a[...] + b[...]


def add(a, b):
    return call(add_body, "add", [VMEM, VMEM], [(a.shape, f32, None)], 8)(a, b)[0]


def sum_copies_body(pieces, out):
    total = pieces[0]
    for k in range(1, pieces.shape[0]):
        total = total + pieces[k]
    for k in range(out.shape[0]):
        out[k] = total


def sum_copies(pieces, copies):
    shape = (copies, *pieces.shape[1:])
    return call(sum_copies_body, "sum_copies", [VMEM], [(shape, f32, None)], 4)(pieces)[0]


def terms_body(pieces, q_prev, factor, out, right):
    merged = pieces[0]
    for k in range(1, N_CHIP):
        merged = merged + pieces[k]
    m_parts = split3(merged)
    left = fold3(mm(jnp.concatenate(m_parts, axis=0), stack3(q_prev[...]), NT))
    left = left[:, :RANK] + left[:, RANK : 2 * RANK] + left[:, 2 * RANK :]
    factor[...] = jnp.concatenate([left[: OWN // 2], left[OWN // 2 :]], axis=1)
    parts = stack3(left.T)
    m1, m2, m3 = m_parts
    right[...] = fold3((mm(parts, m3, NN) + mm(parts, m2, NN)) + mm(parts, m1, NN))
    gram = fold3(mm(parts, parts, NT))
    gram = gram[:, :RANK] + gram[:, RANK : 2 * RANK] + gram[:, 2 * RANK :]
    per = COLS // 2 // LANES
    for r in range(N_REP):
        i, j = divmod(r // 2, per)
        column = LANES * (j + per * (r % 2))
        for k in range(4):
            out[r, k] = right[8 * i + 2 * k : 8 * i + 2 * k + 2, column : column + LANES]
    for p in range(N_CHIP):
        first, second = gram[4 * p : 4 * p + 2], gram[4 * p + 2 : 4 * p + 4]
        both = jnp.concatenate([first, second], axis=1)
        out[2 * p, 4] = both
        out[2 * p + 1, 4] = both


def terms(pieces, q_prev):
    return call(
        terms_body, "terms", [VMEM, VMEM],
        [((OWN // 2, LANES), f32, None), ((N_REP, 5, 2, LANES), f32, None)],
        16, [pltpu.VMEM((RANK, COLS), f32)], cost=100_000_000,
    )(pieces, q_prev.T)


def last_sum_body(pieces, factor, out):
    total = pieces[0]
    for k in range(1, N_FSDP):
        total = total + pieces[k]
    for k in range(N_CHIP):
        for n in range(5):
            out[k, n] = total[n]
        for n in range(8):
            out[k, 5 + n] = factor[2 * n : 2 * n + 2]


def last_sum(pieces, factor):
    return call(
        last_sum_body, "last_sum", [VMEM, VMEM], [((N_CHIP, 13, 2, LANES), f32, None)], 4
    )(pieces, factor)[0]


PANEL = 16


def inverse_triangle(gram):
    eye = (
        lax.broadcasted_iota(jnp.int32, (RANK, RANK), 0)
        == lax.broadcasted_iota(jnp.int32, (RANK, RANK), 1)
    ).astype(f32)
    both = jnp.concatenate([gram, eye], axis=1)
    groups = RANK // 8
    rows = [both[8 * g : 8 * g + 8] for g in range(groups)]
    tile = (8, 2 * RANK)
    sub = lax.broadcasted_iota(jnp.int32, tile, 0)
    pivots = [jnp.ones(tile, f32)] * groups
    for start in range(0, RANK, PANEL):
        columns = [
            {
                g: jnp.broadcast_to(rows[g][:, start + j : start + j + 1], tile)
                for g in range(start // 8, groups)
            }
            for j in range(PANEL)
        ]
        for k in range(PANEL):
            at, line = divmod(start + k, 8)
            pivot = jnp.broadcast_to(columns[k][at][line : line + 1], tile)
            inv = 1.0 / pivot
            pivots[at] = jnp.where(sub == line, pivot, pivots[at])
            scale = {g: c * inv for g, c in columns[k].items() if g >= at}
            scale[at] = jnp.where(sub > line, scale[at], 0.0)
            for j in range(k + 1, PANEL):
                head = jnp.broadcast_to(columns[j][at][line : line + 1], tile)
                for g in scale:
                    columns[j][g] = columns[j][g] - scale[g] * head
            row = jnp.broadcast_to(rows[at][line : line + 1], tile)
            for g in scale:
                rows[g] = rows[g] - scale[g] * row
    done = [row * lax.rsqrt(pivot) for row, pivot in zip(rows, pivots)]
    return jnp.concatenate(done, axis=0)[:, RANK:]


def stacked(sums, p, start, stop):
    return jnp.concatenate([sums[p, n] for n in range(start, stop)], axis=0)


def solve_body(sums, inverse):
    gram = jnp.concatenate(
        [sums[p, 4, :, half : half + RANK] for p in range(N_CHIP) for half in (0, RANK)], axis=0
    )
    inverse[...] = inverse_triangle(gram)


def solve(sums):
    return call(
        solve_body, "solve", [VMEM], [((RANK, RANK), f32, None)], 4, cost=4_000_000_000
    )(sums)[0]


STEP = 128


def final_body(
    core, g_own, e_own, g_other, e_other, sums_own, sums_other, inverse, weight, first, second,
    new_errors, q_next, new_weight, new_first, new_second,
    right, mix, factor, err_buf, weight_buf, first_buf, second_buf, sems,
):
    half = COLS // 2
    for source, place in ((sums_own, core[0]), (sums_other, 1 - core[0])):
        block = jnp.concatenate(
            [
                jnp.concatenate([stacked(source, 2 * i, 0, 4), stacked(source, 2 * i + 1, 0, 4)], axis=1)
                for i in range(RANK // 8)
            ],
            axis=0,
        )
        right[:, pl.ds(pl.multiple_of(place * half, half), half)] = block
        for p in range(N_CHIP):
            n = OWN // 2
            at = pl.multiple_of(place * HALF + OWN * p, OWN)
            both = stacked(source, p, 5, 13)
            factor[pl.ds(at, n)] = both[:, :RANK]
            factor[pl.ds(at + n, n)] = both[:, RANK:]
    q_t = mm(left_pieces(inverse[...]), right_pieces(right[...]), NN) * (1.0 / N_REP)
    q_next[...] = q_t
    mix[...] = right_pieces(mm(left_pieces(inverse[...].T), right_pieces(q_t), NN))

    copies = []
    for step in range(ROWS // STEP):
        other, n = divmod(step * STEP, HALF)
        place = 1 - core[0] if other else core[0]
        grads, errors = (g_other, e_other) if other else (g_own, e_own)
        piece = slice(n, n + STEP)
        rows = pl.ds(pl.multiple_of(place * HALF + n, STEP), STEP)
        approx = mm(left_pieces(factor[rows]), mix[...], NN)
        merged = grads[piece].astype(f32) + errors[piece].astype(f32)
        err_buf[rows] = (merged - approx).astype(bf16)
        first_f = beta_first * first[rows].astype(f32) + (1.0 - beta_first) * approx
        second_f = beta_second * second[rows].astype(f32) + ((1.0 - beta_second) * approx) * approx
        first_buf[rows] = first_f.astype(bf16)
        second_buf[rows] = second_f.astype(bf16)
        root = second_f * lax.rsqrt(second_f) * (1.0 / correct_second) ** 0.5 + epsilon
        ratio = (first_f * (learn_rate / correct_first)) / root
        weight_buf[rows] = weight[rows] * (1.0 - learn_rate * weight_decay) - ratio
        for n, (buf, out) in enumerate(
            (
                (err_buf, new_errors.at[0]),
                (weight_buf, new_weight),
                (first_buf, new_first),
                (second_buf, new_second),
            )
        ):
            copy = pltpu.make_async_copy(buf.at[rows], out.at[rows], sems.at[n, step])
            copy.start()
            copies.append(copy)
    for copy in copies:
        copy.wait()


def final(core, own, other, sums_own, sums_other, inverse, weight, first, second):
    wide = (ROWS, COLS)
    return call(
        final_body, "final", [SMEM] + [VMEM] * 10,
        [
            ((1, *wide), bf16, ANY),
            ((RANK, COLS), f32, VMEM),
            (wide, f32, ANY),
            (wide, bf16, ANY),
            (wide, bf16, ANY),
        ],
        16,
        [
            pltpu.VMEM((RANK, COLS), f32),
            pltpu.VMEM((6 * RANK, COLS), bf16),
            pltpu.VMEM((ROWS, RANK), f32),
            pltpu.VMEM(wide, bf16),
            pltpu.VMEM(wide, f32),
            pltpu.VMEM(wide, bf16),
            pltpu.VMEM(wide, bf16),
            pltpu.SemaphoreType.DMA((4, ROWS // STEP)),
        ],
        cost=400_000_000,
    )(core, *own, *other, sums_own, sums_other, inverse, weight, first, second)


PLANE = [[2 * p + c for p in range(N_CHIP)] for c in range(2)]
SWAP = [(i, i ^ 1) for i in range(N_REP)]


def exchange(x):
    return lax.all_to_all(x, "rep", 0, 0, axis_index_groups=PLANE)


def swap(x):
    return lax.ppermute(x, "rep", SWAP)


def shards(grads, errors, q_prev, weight, first_moment, second_moment):
    core = (lax.axis_index("rep") % 2).astype(jnp.int32).reshape(1)
    theirs, *other = merge_half(True, core, grads, errors)
    arrived = swap(theirs)
    mine, *own, weight = merge_half(False, core, grads, errors, weight)
    pieces = exchange(add(mine, arrived).reshape(N_CHIP, OWN, COLS))
    factor, right = terms(pieces, q_prev)
    pieces = sum_copies(lax.all_to_all(right, "rep", 0, 0), N_FSDP)
    pieces = last_sum(lax.all_to_all(pieces, "fsdp", 0, 0), factor)
    sums_own = exchange(pieces)
    sums_other = swap(sums_own)
    inverse = solve(sums_own)
    outs = final(
        core, own, other, sums_own, sums_other, inverse, weight, first_moment, second_moment
    )
    return outs[0], outs[1].T, *outs[2:]


def solution(mesh):
    return jax.shard_map(
        shards,
        mesh=mesh,
        in_specs=(
            P("rep", "fsdp", None),
            P("rep", "fsdp", None),
            P(),
            P("fsdp", None),
            P("fsdp", None),
            P("fsdp", None),
        ),
        out_specs=(P("rep", "fsdp", None), P(), P("fsdp", None), P("fsdp", None), P("fsdp", None)),
        check_vma=False,
    )
```
